32 devices in a mesh: groups: 2 (over y), pair: 4 (over x, core), tensor: 4 (over z).
Axes of the slice: x: 2, y: 2, z: 4, core: 2. Of those that a mesh axis runs over, the one named last changes fastest.
Arguments:
- x_clean: bfloat16 [1024, 8192], P('groups', 'pair'), parts along dimension 0, may hold values from -6 to 6
- x_corr: bfloat16 [1024, 8192], P('groups', 'pair'), parts along dimension 0, may hold values from -6 to 6
- cotangent: bfloat16 [1024, 8192], P('groups', 'pair'), parts along dimension 0, may hold values from -6 to 6
- w_gate: bfloat16 [8192, 14336], P('pair', 'tensor'), may hold values from -0.0625 to 0.0625
- w_up: bfloat16 [8192, 14336], P('pair', 'tensor'), may hold values from -0.0625 to 0.0625
- w_down: bfloat16 [14336, 8192], P('tensor', 'pair'), may hold values from -0.0625 to 0.0625
- start: int32 [64], P(('groups', 'pair')), parts along dimension 0, may hold values from 0 to 7
- partners: int32 [64, 3], P(('groups', 'pair')), parts along dimension 0, may hold values from -1 to 31, as said below
Outputs:
- scores: float32 [64, 14336], P(('groups', 'pair'), 'tensor'), parts along dimension 0
- input_grad: bfloat16 [1024, 8192], P('groups', 'pair'), parts along dimension 0
The draws below stay inside these ranges and needn't reach their ends.
There are 2 independent parts, one for each index of `groups`. The reference program is written for one: setup_inputs(seed, part) draws one part's arguments, and reference() takes and returns one part's arrays. A program takes and returns all parts, laid end to end along the dimension named above; an argument that names none is the same for every part. Nothing has to cross between parts.
Inputs may be any that keep to these rules, and one draw needn't show every extreme that they name: Each clean prompt has 1 to 3 partners in its first slots and -1 in the rest; every corrupted prompt is the first partner of exactly one clean prompt; a partner may repeat within a prompt's slots.
All inputs are finite; a program needn't handle non-finite values.
Results may differ from the reference program's by a relative error of at most 0.02.
Values may be sent and summed in bfloat16 or wider, within the bound.
A program may use at most 192 MiB of HBM per device.

```python
import jax
import jax.numpy as jnp
from jax import lax

D = 8192
FF = 14336
SEQ = 16
MAXP = 3
PROMPTS = 32
TOKENS = 512
N_PAIR = 4


def draw_partners(key, part):
    key = jax.random.fold_in(key, 11)
    key_first, key_extra, key_count = jax.random.split(key, 3)
    first = jax.random.permutation(key_first, PROMPTS).astype(jnp.int32)
    extra = jax.random.randint(key_extra, (PROMPTS, MAXP - 1), 0, PROMPTS, dtype=jnp.int32)
    count = jax.random.randint(key_count, (PROMPTS,), 1, MAXP + 1, dtype=jnp.int32)
    count = count.at[0].set(1).at[1].set(MAXP)
    ids = jnp.concatenate([first[:, None], extra], axis=1)
    slot = jnp.arange(MAXP, dtype=jnp.int32)[None, :]
    return jnp.where(slot < count[:, None], ids, -1).astype(jnp.int32)


def place_ends(values, own_key, smallest, top_value):
    index_at = [jax.random.randint(jax.random.fold_in(own_key, axis), (), 0, length) for axis, length in enumerate(values.shape)]
    longest = values.shape.index(max(values.shape))
    next_to = index_at[:longest] + [(index_at[longest] + 1) % values.shape[longest]] + index_at[longest + 1:]
    return values.at[tuple(index_at)].set(smallest).at[tuple(next_to)].set(top_value)


def with_spikes(values, rng, source, target, blocks, factor):
    def block_of(dim):
        return (jnp.arange(values.shape[dim]) // (values.shape[dim] // blocks)).reshape((-1,) + (1,) * (values.ndim - 1 - dim))

    near = jax.random.permutation(rng, blocks)[block_of(target)]
    far = (block_of(target) + blocks // 2) % blocks
    return jnp.where((block_of(source) == near) | (block_of(source) == far), factor * values, values)


def block_levels(rng, extent, cuts, low, high):
    def one(axis_at, shards_of):
        steps = jax.random.uniform(jax.random.fold_in(jax.random.fold_in(rng, 6), axis_at), (shards_of,), jnp.float32, low / len(cuts), high / len(cuts))
        return jnp.repeat(jnp.exp(steps), extent[axis_at] // shards_of).reshape((-1,) + (1,) * (len(extent) - axis_at - 1))

    gain = one(*cuts[0])
    for cut in cuts[1:]:
        gain = gain * one(*cut)
    return gain


def noise(own_key, dims, scale, reach, cuts=(), kind=jnp.bfloat16):
    entries = scale * jax.random.normal(own_key, dims, jnp.float32)
    if cuts:
        entries = entries * block_levels(own_key, dims, cuts, -0.22, 0.18)
    return jnp.clip(entries, -reach, reach).astype(kind)


def heavy_noise(key, shape, deviation, limit, cuts, heavy, kind=jnp.bfloat16):
    drawn = deviation * jax.random.normal(key, shape, jnp.float32)
    if cuts:
        drawn = drawn * block_levels(key, shape, cuts, -0.22, 0.18)
    return jnp.clip(with_spikes(drawn, jax.random.fold_in(key, 3), *heavy), -limit, limit).astype(kind)


def setup_inputs(seed: int = 0, part: int = 0) -> dict:
    splits = jax.random.split(jax.random.key(seed), 9)
    own_keys = jax.random.split(jax.random.fold_in(splits[8], part), 9)
    x_clean = noise(own_keys[0], (TOKENS, D), 1.0, 6.0, ((1, 4),))
    x_corr = noise(own_keys[1], (TOKENS, D), 1.0, 6.0, ((1, 4),))
    cotangent = heavy_noise(own_keys[2], (TOKENS, D), 1.0, 6.0, ((1, 4),), (1, 0, 4, 2.0))
    w_gate = noise(splits[3], (D, FF), D ** -0.5, 0.0625, ((0, 4), (1, 4)))
    w_up = noise(splits[4], (D, FF), D ** -0.5, 0.0625, ((0, 4), (1, 4)))
    w_down = noise(splits[5], (FF, D), D ** -0.5, 0.0625, ((0, 4), (1, 4)))
    start = place_ends(jax.random.randint(own_keys[6], (PROMPTS,), 0, SEQ // 2), jax.random.fold_in(own_keys[6], 1), 0, (SEQ // 2) - 1).astype(jnp.int32)
    partners = draw_partners(jax.random.fold_in(jax.random.fold_in(splits[8], part), 71), part)
    return dict(x_clean=x_clean, x_corr=x_corr, cotangent=cotangent, w_gate=w_gate, w_up=w_up, w_down=w_down, start=start, partners=partners)


def silu_grad(value):
    sig = jax.nn.sigmoid(value)
    return sig * (1.0 + value * (1.0 - sig))

def block_sum(left, right):
    width = D // N_PAIR
    total = jnp.zeros((left.shape[0], right.shape[1]), jnp.float32)
    for block in range(N_PAIR):
        piece = jnp.dot(left[:, block * width:(block + 1) * width], right[block * width:(block + 1) * width], preferred_element_type=jnp.float32)
        total = total + lax.optimization_barrier(piece.astype(jnp.bfloat16)).astype(jnp.float32)
    return total

def reference(x_clean, x_corr, cotangent, w_gate, w_up, w_down, start, partners):
    gate_c = block_sum(x_clean, w_gate)
    up_c = block_sum(x_clean, w_up)
    gate_r = block_sum(x_corr, w_gate)
    up_r = block_sum(x_corr, w_up)
    grad_h = block_sum(cotangent, w_down.T)
    h_c = jax.nn.silu(gate_c) * up_c
    h_r = (jax.nn.silu(gate_r) * up_r).astype(jnp.bfloat16)
    d_gate = (grad_h * up_c * silu_grad(gate_c)).astype(jnp.bfloat16)
    d_up = (grad_h * jax.nn.silu(gate_c)).astype(jnp.bfloat16)
    input_grad = (jnp.dot(d_gate, w_gate.T, preferred_element_type=jnp.float32) + jnp.dot(d_up, w_up.T, preferred_element_type=jnp.float32)).astype(jnp.bfloat16)
    valid = (partners >= 0).astype(jnp.float32)
    safe = jnp.maximum(partners, 0).astype(jnp.int32)
    corr_all = h_r.reshape(PROMPTS, SEQ, FF)
    total = jnp.zeros((PROMPTS, SEQ, FF), jnp.float32)
    for slot in range(MAXP):
        total = total + valid[:, slot][:, None, None] * corr_all[safe[:, slot]].astype(jnp.float32)
    count = lax.optimization_barrier(jnp.sum(valid, axis=1))
    delta = total - count[:, None, None] * h_c.reshape(PROMPTS, SEQ, FF)
    position = jnp.arange(SEQ, dtype=jnp.int32)
    keep = (position[None, :] >= start[:, None]).astype(jnp.float32)
    scores = lax.optimization_barrier(jnp.sum(keep[:, :, None] * delta * grad_h.reshape(PROMPTS, SEQ, FF), axis=1)) / SEQ
    return (scores, input_grad)
```

```python
import jax
import jax.numpy as jnp
from jax import lax
from jax.sharding import PartitionSpec as P

SEQ = 16
CHUNKS = 2


def silu_grad(value):
    sig = jax.nn.sigmoid(value)
    return sig * (1.0 + value * (1.0 - sig))


def make_body(n_pair):
    chips = n_pair // 2
    to_core = [(q, q ^ 1) for q in range(n_pair)]

    def to_chip(shift):
        return [(q, ((q // 2 + shift) % chips) * 2 + q % 2) for q in range(n_pair)]

    def columns(value, at, width):
        return lax.dynamic_slice_in_dim(value, at * width, width, axis=1)

    def body(x_clean, x_corr, cotangent, w_gate, w_up, w_down, start, partners):
        tokens = x_clean.shape[0]
        neurons = w_gate.shape[1]
        half = neurons // 2
        block = half // chips
        index = lax.axis_index("pair")
        core = index % 2
        chip = index // 2
        transposed = (((1,), (1,)), ((), ()))

        def reduce(part):
            arrived = lax.ppermute(columns(part, 1 - core, half), "pair", to_core)
            local = columns(part, core, half).astype(jnp.float32) + arrived.astype(jnp.float32)
            local = local.astype(jnp.bfloat16)
            total = columns(local, chip, block).astype(jnp.float32)
            for shift in range(1, chips):
                piece = columns(local, (chip + shift) % chips, block)
                total = total + lax.ppermute(piece, "pair", to_chip(shift)).astype(jnp.float32)
            return total

        def gather(own):
            rows = own.shape[0]
            mine = jnp.zeros((rows, half), own.dtype)
            mine = lax.dynamic_update_slice_in_dim(mine, own, chip * block, axis=1)
            for shift in range(1, chips):
                piece = lax.ppermute(own, "pair", to_chip(shift))
                source = (chip - shift + chips) % chips
                mine = lax.dynamic_update_slice_in_dim(mine, piece, source * block, axis=1)
            other = lax.ppermute(mine, "pair", to_core)
            first = core == 0
            return jnp.concatenate(
                [jnp.where(first, mine, other), jnp.where(first, other, mine)], axis=1
            )

        def project(left, weight):
            return jnp.dot(left, weight, preferred_element_type=jnp.float32).astype(jnp.bfloat16)

        def project_back(left, weight):
            return lax.dot_general(
                left, weight, transposed, preferred_element_type=jnp.float32
            ).astype(jnp.bfloat16)

        partners_all = lax.all_gather(partners, "pair", axis=0, tiled=True)
        start_all = lax.all_gather(start, "pair", axis=0, tiled=True)

        rows = tokens // CHUNKS
        summed = []
        for k in range(CHUNKS):
            at = slice(k * rows, (k + 1) * rows)
            gate_c = reduce(project(x_clean[at], w_gate))
            up_c = reduce(project(x_clean[at], w_up))
            grad_h = reduce(project_back(cotangent[at], w_down))
            summed.append((gate_c, up_c, grad_h))

        acts, grads, out = [], [], []
        for gate_c, up_c, grad_h in summed:
            silu_c = jax.nn.silu(gate_c)
            acts.append(silu_c * up_c)
            grads.append(grad_h)
            d_gate = gather((grad_h * up_c * silu_grad(gate_c)).astype(jnp.bfloat16))
            d_up = gather((grad_h * silu_c).astype(jnp.bfloat16))
            partial = lax.dot_general(
                d_gate, w_gate, transposed, preferred_element_type=jnp.float32
            )
            partial = partial + lax.dot_general(
                d_up, w_up, transposed, preferred_element_type=jnp.float32
            )
            partial = partial.astype(jnp.bfloat16)
            if out:
                partial, out[-1] = lax.optimization_barrier((partial, out[-1]))
            out.append(lax.psum(partial, "tensor"))
        input_grad = jnp.concatenate(out, axis=0)

        gate_r = reduce(project(x_corr, w_gate))
        up_r = reduce(project(x_corr, w_up))
        act_r = (jax.nn.silu(gate_r) * up_r).astype(jnp.bfloat16)
        act_c = jnp.concatenate(acts, axis=0)
        grad_h = jnp.concatenate(grads, axis=0)

        prompts = tokens // SEQ
        row = jnp.arange(tokens, dtype=jnp.int32)
        used = (partners_all >= 0).astype(jnp.float32)
        mixing = jnp.zeros((tokens, tokens), jnp.float32)
        for slot in range(partners.shape[1]):
            picked = jnp.repeat(partners_all[:, slot], SEQ)
            wanted = jnp.where(picked >= 0, picked * SEQ + row % SEQ, -1)
            mixing = mixing + (wanted[:, None] == row[None, :]).astype(jnp.float32)
        total = jnp.dot(mixing.astype(jnp.bfloat16), act_r, preferred_element_type=jnp.float32)
        count = jnp.repeat(jnp.sum(used, axis=1), SEQ)
        keep = (row % SEQ >= jnp.repeat(start_all, SEQ)).astype(jnp.float32)
        weighted = keep[:, None] * (total - count[:, None] * act_c) * grad_h
        own = jnp.sum(weighted.reshape(prompts, SEQ, block), axis=1) / SEQ
        share = prompts // n_pair
        placed = lax.all_to_all(
            own.reshape(n_pair, share, block), "pair", split_axis=0, concat_axis=0, tiled=True
        )
        placed = placed.reshape(chips, 2, share, block)
        scores = placed.transpose(2, 1, 0, 3).reshape(share, neurons)
        return (scores, input_grad)

    return body


def solution(mesh):
    placed = (
        P("groups", "pair"),
        P("groups", "pair"),
        P("groups", "pair"),
        P("pair", "tensor"),
        P("pair", "tensor"),
        P("tensor", "pair"),
        P(("groups", "pair")),
        P(("groups", "pair"), None),
    )
    return jax.shard_map(
        make_body(mesh.shape["pair"]),
        mesh=mesh,
        in_specs=placed,
        out_specs=(P(("groups", "pair"), "tensor"), P("groups", "pair")),
        check_vma=False,
    )
```

```python
import jax
import jax.numpy as jnp
from jax import lax
from jax.experimental import pallas as pl
from jax.experimental.pallas import tpu as pltpu
from jax.sharding import PartitionSpec as P

SEQ = 16
CHUNKS = 2
VMEM_BYTES = 64 * 2**20 - 2**18


def silu_grad(value):
    sig = jax.nn.sigmoid(value)
    return sig * (1.0 + value * (1.0 - sig))


def make_body(n_pair):
    chips = n_pair // 2
    to_core = [(q, q ^ 1) for q in range(n_pair)]

    def to_chip(shift):
        return [(q, ((q // 2 + shift) % chips) * 2 + q % 2) for q in range(n_pair)]

    def columns(value, at, width):
        return lax.dynamic_slice_in_dim(value, at * width, width, axis=1)

    def body(x_clean, x_corr, cotangent, w_gate, w_up, w_down, start, partners):
        tokens = x_clean.shape[0]
        neurons = w_gate.shape[1]
        half = neurons // 2
        block = half // chips
        index = lax.axis_index("pair")
        core = index % 2
        chip = index // 2
        transposed = (((1,), (1,)), ((), ()))

        def reduce(part):
            arrived = lax.ppermute(columns(part, 1 - core, half), "pair", to_core)
            local = columns(part, core, half).astype(jnp.float32) + arrived.astype(jnp.float32)
            local = local.astype(jnp.bfloat16)
            total = columns(local, chip, block).astype(jnp.float32)
            for shift in range(1, chips):
                piece = columns(local, (chip + shift) % chips, block)
                total = total + lax.ppermute(piece, "pair", to_chip(shift)).astype(jnp.float32)
            return total

        def gather(own):
            rows = own.shape[0]
            mine = jnp.zeros((rows, half), own.dtype)
            mine = lax.dynamic_update_slice_in_dim(mine, own, chip * block, axis=1)
            for shift in range(1, chips):
                piece = lax.ppermute(own, "pair", to_chip(shift))
                source = (chip - shift + chips) % chips
                mine = lax.dynamic_update_slice_in_dim(mine, piece, source * block, axis=1)
            other = lax.ppermute(mine, "pair", to_core)
            first = core == 0
            return jnp.concatenate(
                [jnp.where(first, mine, other), jnp.where(first, other, mine)], axis=1
            )

        def project(left, weight):
            return jnp.dot(left, weight, preferred_element_type=jnp.float32).astype(jnp.bfloat16)

        def project_back(left, weight):
            return lax.dot_general(
                left, weight, transposed, preferred_element_type=jnp.float32
            ).astype(jnp.bfloat16)

        partners_all = lax.all_gather(partners, "pair", axis=0, tiled=True)
        start_all = lax.all_gather(start, "pair", axis=0, tiled=True)

        rows = tokens // CHUNKS
        summed = []
        for k in range(CHUNKS):
            at = slice(k * rows, (k + 1) * rows)
            gate_c = reduce(project(x_clean[at], w_gate))
            up_c = reduce(project(x_clean[at], w_up))
            grad_h = reduce(project_back(cotangent[at], w_down))
            summed.append((gate_c, up_c, grad_h))

        acts, grads, out = [], [], []
        for gate_c, up_c, grad_h in summed:
            silu_c = jax.nn.silu(gate_c)
            acts.append(silu_c * up_c)
            grads.append(grad_h)
            d_gate = gather((grad_h * up_c * silu_grad(gate_c)).astype(jnp.bfloat16))
            d_up = gather((grad_h * silu_c).astype(jnp.bfloat16))
            partial = lax.dot_general(
                d_gate, w_gate, transposed, preferred_element_type=jnp.float32
            )
            partial = partial + lax.dot_general(
                d_up, w_up, transposed, preferred_element_type=jnp.float32
            )
            partial = partial.astype(jnp.bfloat16)
            if out:
                partial, out[-1] = lax.optimization_barrier((partial, out[-1]))
            out.append(lax.psum(partial, "tensor"))
        input_grad = jnp.concatenate(out, axis=0)

        gate_r = reduce(project(x_corr, w_gate))
        up_r = reduce(project(x_corr, w_up))
        act_r = (jax.nn.silu(gate_r) * up_r).astype(jnp.bfloat16)
        act_c = jnp.concatenate(acts, axis=0)
        grad_h = jnp.concatenate(grads, axis=0)

        prompts = tokens // SEQ
        row = jnp.arange(tokens, dtype=jnp.int32)
        used = (partners_all >= 0).astype(jnp.float32)
        mixing = jnp.zeros((tokens, tokens), jnp.float32)
        for slot in range(partners.shape[1]):
            picked = jnp.repeat(partners_all[:, slot], SEQ)
            wanted = jnp.where(picked >= 0, picked * SEQ + row % SEQ, -1)
            mixing = mixing + (wanted[:, None] == row[None, :]).astype(jnp.float32)
        total = jnp.dot(mixing.astype(jnp.bfloat16), act_r, preferred_element_type=jnp.float32)
        count = jnp.repeat(jnp.sum(used, axis=1), SEQ)
        keep = (row % SEQ >= jnp.repeat(start_all, SEQ)).astype(jnp.float32)
        weighted = keep[:, None] * (total - count[:, None] * act_c) * grad_h
        own = jnp.sum(weighted.reshape(prompts, SEQ, block), axis=1) / SEQ
        share = prompts // n_pair
        placed = lax.all_to_all(
            own.reshape(n_pair, share, block), "pair", split_axis=0, concat_axis=0, tiled=True
        )
        placed = placed.reshape(chips, 2, share, block)
        scores = placed.transpose(2, 1, 0, 3).reshape(share, neurons)
        return (scores, input_grad)

    return body


TILE = 256
SLOTS = 2
MESH = pl.DeviceIdType.MESH
F32 = jnp.float32
BF16 = jnp.bfloat16


def fused(
    x_clean, x_corr, cotangent, start, partners, w_gate, w_up, w_down,
    scores, input_grad,
    ring_n, ring_t, ring_b, core_out, core_in, sums, chip_in, grads, part, half_in, quarter_in,
    act_c, grad_h, act_r, mixing, scale, table, own_scores,
    ring_n_sem, ring_t_sem, ring_b_sem, core_out_sem, core_in_sem, chip_out_sem, chip_in_sem,
    dx_out, dx_in, dc_out, dc_in, z_out, z_in, table_out, table_in, score_out, score_in,
):
    tokens, width = x_clean.shape
    rows = tokens // CHUNKS
    neurons = w_gate.shape[1]
    half = neurons // 2
    block = half // 2
    share = partners.shape[0]
    prompts = tokens // SEQ
    index = lax.axis_index("pair")
    depth = lax.axis_index("tensor")
    core = lax.rem(index, 2)
    chip = index // 2
    sibling = chip * 2 + (1 - core)
    across = (1 - chip) * 2 + core
    diagonal = (1 - chip) * 2 + (1 - core)
    others = (sibling, across, diagonal)
    odd = lax.rem(depth, 2)
    high = depth // 2
    z_near = high * 2 + (1 - odd)
    z_far = (1 - high) * 2 + odd
    mine = core * 2 + chip
    transposed = (((1,), (1,)), ((), ()))

    def remote(src, dst, send, recv, **where):
        return pltpu.make_async_remote_copy(
            src_ref=src, dst_ref=dst, send_sem=send, recv_sem=recv,
            device_id=where, device_id_type=MESH,
        )

    barrier = pltpu.get_barrier_semaphore()
    for other in others:
        pl.semaphore_signal(barrier, inc=1, device_id={"pair": other}, device_id_type=MESH)
    for other in (z_near, z_far):
        pl.semaphore_signal(barrier, inc=1, device_id={"tensor": other}, device_id_type=MESH)

    units = []
    for k in range(CHUNKS):
        units += [(x_clean, w_gate, False, k), (x_clean, w_up, False, k), (cotangent, w_down, True, k)]
    for k in range(CHUNKS):
        units += [(x_corr, w_gate, False, k), (x_corr, w_up, False, k)]
    tiles = half // TILE

    def tile_copy(u, side, parity, i):
        _, weight, flipped, _ = units[u]
        at = pl.ds(pl.multiple_of(side * half + i * TILE, TILE), TILE)
        slot = parity * SLOTS + lax.rem(i, SLOTS)
        if flipped:
            return pltpu.make_async_copy(weight.at[at, :], ring_t.at[slot], ring_t_sem.at[slot])
        return pltpu.make_async_copy(weight.at[:, at], ring_n.at[slot], ring_n_sem.at[slot])

    stages = [("out", 0)]
    for u in range(len(units)):
        if u + 1 < len(units):
            stages.append(("out", u + 1))
        stages.append(("own", u))
    flow = {"at": 0}

    def side_of(kind):
        return 1 - core if kind == "out" else core

    def prefetch(s):
        if s < len(stages):
            kind, u = stages[s]
            for i in range(SLOTS):
                tile_copy(u, side_of(kind), s % 2, jnp.int32(i)).start()

    def core_copy(u):
        return remote(
            core_out.at[u % 2], core_in.at[u % 4], core_out_sem.at[u % 2], core_in_sem.at[u % 4],
            pair=sibling,
        )

    def chip_copy(u):
        at = pl.ds(pl.multiple_of((1 - chip) * block, 128), block)
        return remote(
            sums.at[u, :, at], chip_in.at[u], chip_out_sem.at[u], chip_in_sem.at[u], pair=across
        )

    def stage():
        s = flow["at"]
        flow["at"] = s + 1
        kind, u = stages[s]
        left, _, flipped, k = units[u]
        prefetch(s + 1)
        if kind == "out" and u >= 2:
            core_copy(u - 2).wait_send()
        if kind == "own":
            core_copy(u).wait_recv()

        def step(i, carry):
            tile_copy(u, side_of(kind), s % 2, i).wait()
            slot = (s % 2) * SLOTS + lax.rem(i, SLOTS)
            at = pl.ds(pl.multiple_of(i * TILE, TILE), TILE)
            lhs = left[k * rows:(k + 1) * rows, :]
            if flipped:
                value = lax.dot_general(lhs, ring_t[slot], transposed, preferred_element_type=F32)
            else:
                value = jnp.dot(lhs, ring_n[slot], preferred_element_type=F32)
            if kind == "out":
                core_out[u % 2, :, at] = value.astype(BF16)
            else:
                value = value + core_in[u % 4, :, at].astype(F32)
                sums[u, :, at] = value.astype(BF16)

            @pl.when(i + SLOTS < tiles)
            def _():
                tile_copy(u, side_of(kind), s % 2, i + SLOTS).start()

            return carry

        lax.fori_loop(0, tiles, step, 0)
        if kind == "out":
            core_copy(u).start()

    def run_to(u):
        while stages[flow["at"] - 1] != ("own", u) or flow["at"] == 0:
            stage()

    own_at = pl.ds(pl.multiple_of(chip * block, 128), block)

    def total(u, at):
        return sums[u, at, own_at].astype(F32) + chip_in[u, at, :].astype(F32)

    def grad_copy(k, a):
        return remote(
            grads.at[k, a, mine], grads.at[k, a, mine], dx_out.at[2 * k + a], dx_in.at[2 * k + a],
            pair=across,
        )

    def grad_share(k, a):
        at = pl.ds(core * 2, 2)
        return remote(
            grads.at[k, a, at], grads.at[k, a, at], dc_out.at[2 * k + a], dc_in.at[2 * k + a],
            pair=sibling,
        )

    def finish_clean(k):
        for u in range(3 * k, 3 * k + 3):
            chip_copy(u).wait_recv()

        def step(i, carry):
            at = pl.ds(pl.multiple_of(i * 16, 16), 16)
            gate, up, grad = (total(3 * k + j, at) for j in range(3))
            sig = jax.nn.sigmoid(gate)
            silu = gate * sig
            grads[k, 0, mine, at, :] = (grad * up * (sig * (1.0 + gate * (1.0 - sig)))).astype(BF16)
            grads[k, 1, mine, at, :] = (grad * silu).astype(BF16)
            place = pl.ds(pl.multiple_of(k * rows + i * 16, 16), 16)
            act_c[place, :] = silu * up
            grad_h[place, :] = grad
            return carry

        lax.fori_loop(0, rows // 16, step, 0)
        for a in range(2):
            grad_copy(k, a).start()

    def finish_corr(k):
        first = 3 * CHUNKS + 2 * k
        for u in (first, first + 1):
            chip_copy(u).wait_recv()

        def step(i, carry):
            at = pl.ds(pl.multiple_of(i * 16, 16), 16)
            gate, up = total(first, at), total(first + 1, at)
            place = pl.ds(pl.multiple_of(k * rows + i * 16, 16), 16)
            act_r[place, :] = (gate * jax.nn.sigmoid(gate) * up).astype(BF16)
            return carry

        lax.fori_loop(0, rows // 16, step, 0)

    def back_copy(a, i):
        slot = lax.rem(i, SLOTS)
        at = pl.ds(pl.multiple_of(i * TILE, TILE), TILE)
        weight = (w_gate, w_up)[a]
        return pltpu.make_async_copy(
            weight.at[at, :], ring_b.at[a, slot], ring_b_sem.at[a, slot]
        )

    def back(k):
        steps = width // TILE
        for i in range(SLOTS):
            for a in range(2):
                back_copy(a, jnp.int32(i)).start()
        for a in range(2):
            grad_copy(k, a).wait_recv()
            grad_share(k, a).start()
        for a in range(2):
            grad_share(k, a).wait_recv()

        def step(i, carry):
            slot = lax.rem(i, SLOTS)
            value = jnp.zeros((rows, TILE), F32)
            for a in range(2):
                back_copy(a, i).wait()
                for b in range(4):
                    value = value + lax.dot_general(
                        grads[k, a, b], ring_b[a, slot, :, b * block:(b + 1) * block],
                        transposed, preferred_element_type=F32,
                    )
            part[k, :, pl.ds(pl.multiple_of(i * TILE, TILE), TILE)] = value.astype(BF16)

            @pl.when(i + SLOTS < steps)
            def _():
                for a in range(2):
                    back_copy(a, i + SLOTS).start()

            return carry

        lax.fori_loop(0, steps, step, 0)

    half_rows = rows // 2
    quarter_rows = rows // 4

    def z_copy(k, n):
        sems = z_out.at[4 * k + n], z_in.at[4 * k + n]
        if n == 0:
            at = pl.ds(pl.multiple_of((1 - odd) * half_rows, 16), half_rows)
            return remote(part.at[k, at, :], half_in.at[k], *sems, tensor=z_near)
        if n == 1:
            at = pl.ds(
                pl.multiple_of(odd * half_rows + (1 - high) * quarter_rows, 16), quarter_rows
            )
            return remote(part.at[k, at, :], quarter_in.at[k], *sems, tensor=z_far)
        if n == 2:
            at = pl.ds(
                pl.multiple_of(k * rows + odd * half_rows + high * quarter_rows, 16), quarter_rows
            )
            return remote(input_grad.at[at, :], input_grad.at[at, :], *sems, tensor=z_far)
        at = pl.ds(pl.multiple_of(k * rows + odd * half_rows, 16), half_rows)
        return remote(input_grad.at[at, :], input_grad.at[at, :], *sems, tensor=z_near)

    def z_step(k, n):
        z_copy(k, n).wait_recv()
        if n == 0:
            z_copy(k, n).wait_send()

            def step(i, carry):
                at = pl.ds(pl.multiple_of(odd * half_rows + i * 16, 16), 16)
                here = pl.ds(pl.multiple_of(i * 16, 16), 16)
                part[k, at, :] = (
                    part[k, at, :].astype(F32) + half_in[k, here, :].astype(F32)
                ).astype(BF16)
                return carry

            lax.fori_loop(0, half_rows // 16, step, 0)
        if n == 1:

            def step(i, carry):
                local = odd * half_rows + high * quarter_rows + i * 16
                at = pl.ds(pl.multiple_of(local, 16), 16)
                place = pl.ds(pl.multiple_of(k * rows + local, 16), 16)
                here = pl.ds(pl.multiple_of(i * 16, 16), 16)
                input_grad[place, :] = (
                    part[k, at, :].astype(F32) + quarter_in[k, here, :].astype(F32)
                ).astype(BF16)
                return carry

            lax.fori_loop(0, quarter_rows // 16, step, 0)
        if n < 3:
            z_copy(k, n + 1).start()

    def table_copy(n):
        return remote(
            table.at[index], table.at[index], table_out.at[n], table_in.at[n], pair=others[n]
        )

    def score_copy(n):
        at = pl.ds(pl.multiple_of(mine * block, 128), block)
        return remote(
            own_scores.at[others[n]], scores.at[:, at], score_out.at[n], score_in.at[n],
            pair=others[n],
        )

    prefetch(0)
    lane = lax.broadcasted_iota(jnp.int32, (share, 128), 1)
    counts = jnp.zeros((share, 128), F32)
    used = jnp.zeros((share, 1), F32)
    for slot in range(partners.shape[1]):
        picked = partners[:, slot:slot + 1]
        counts = counts + (lane == picked).astype(F32)
        used = used + (picked >= 0).astype(F32)
    counts = jnp.where(lane == 126, start[...].astype(F32), counts)
    table[index] = jnp.where(lane == 127, used, counts)
    pl.semaphore_wait(barrier, 5)
    for n in range(3):
        table_copy(n).start()

    last_clean = 3 * CHUNKS - 1
    for u in range(last_clean + 1):
        run_to(u)
        chip_copy(u).start()

    for n in range(3):
        table_copy(n).wait_recv()
    spread = (
        lax.broadcasted_iota(jnp.int32, (tokens, prompts), 0) // SEQ
        == lax.broadcasted_iota(jnp.int32, (tokens, prompts), 1)
    ).astype(BF16)
    by_row = jnp.dot(
        spread, table[...].reshape(prompts, 128).astype(BF16), preferred_element_type=F32
    )
    position = lax.rem(lax.broadcasted_iota(jnp.int32, (tokens, 1), 0), SEQ)
    keep = (position.astype(F32) >= by_row[:, 126:127]).astype(F32)
    scale[...] = jnp.broadcast_to(keep * by_row[:, 127:128], (tokens, 128))
    widen = (
        lax.broadcasted_iota(jnp.int32, (128, tokens), 1) // SEQ
        == lax.broadcasted_iota(jnp.int32, (128, tokens), 0)
    ).astype(BF16)
    wide = jnp.dot((keep * by_row).astype(BF16), widen, preferred_element_type=F32)
    same = position == lax.rem(lax.broadcasted_iota(jnp.int32, (tokens, tokens), 1), SEQ)
    mixing[...] = jnp.where(same, wide, 0.0).astype(BF16)

    finish_clean(0)
    first_corr = 3 * CHUNKS
    run_to(first_corr + 1)
    finish_clean(1)
    run_to(first_corr + 3)
    back(0)
    z_copy(0, 0).start()
    chip_copy(first_corr).start()
    chip_copy(first_corr + 1).start()
    back(1)
    z_copy(1, 0).start()
    chip_copy(first_corr + 2).start()
    chip_copy(first_corr + 3).start()
    z_step(0, 0)
    z_step(0, 1)
    z_step(1, 0)
    z_step(0, 2)
    z_step(1, 1)
    finish_corr(0)
    z_step(1, 2)
    finish_corr(1)

    span = share * SEQ

    def score_step(i, carry):
        at = pl.ds(pl.multiple_of(i * span, span), span)
        mixed = jnp.dot(mixing[at, :], act_r[...], preferred_element_type=F32)
        value = (mixed - scale[at, 0:1] * act_c[at, :]) * grad_h[at, :]
        own_scores[i] = jnp.sum(value.reshape(share, SEQ, block), axis=1) * (1.0 / SEQ)
        return carry

    lax.fori_loop(0, prompts // share, score_step, 0)
    for n in range(3):
        score_copy(n).start()
    scores[:, pl.ds(pl.multiple_of(mine * block, 128), block)] = own_scores[index]

    z_copy(0, 3).wait_recv()
    z_copy(1, 3).wait_recv()
    for n in range(3):
        score_copy(n).wait()
        table_copy(n).wait_send()
    for u in (len(units) - 2, len(units) - 1):
        core_copy(u).wait_send()
    for u in range(len(units)):
        chip_copy(u).wait_send()
    for k in range(CHUNKS):
        for a in range(2):
            grad_copy(k, a).wait_send()
            grad_share(k, a).wait_send()
        for n in range(1, 4):
            z_copy(k, n).wait_send()


def fused_body(x_clean, x_corr, cotangent, w_gate, w_up, w_down, start, partners):
    tokens, width = x_clean.shape
    neurons = w_gate.shape[1]
    rows, half = tokens // CHUNKS, neurons // 2
    block = half // 2
    share = start.shape[0]
    prompts = tokens // SEQ
    units = 5 * CHUNKS
    vmem = pl.BlockSpec(memory_space=pltpu.VMEM)
    anywhere = pl.BlockSpec(memory_space=pl.ANY)
    dma = pltpu.SemaphoreType.DMA
    scores, input_grad = pl.pallas_call(
        fused,
        out_shape=(
            jax.ShapeDtypeStruct((share, neurons), F32),
            jax.ShapeDtypeStruct((tokens, width), BF16),
        ),
        in_specs=[vmem] * 5 + [anywhere] * 3,
        out_specs=(vmem, vmem),
        scratch_shapes=[
            pltpu.VMEM((2 * SLOTS, width, TILE), BF16),
            pltpu.VMEM((2 * SLOTS, TILE, width), BF16),
            pltpu.VMEM((2, SLOTS, TILE, neurons), BF16),
            pltpu.VMEM((2, rows, half), BF16),
            pltpu.VMEM((4, rows, half), BF16),
            pltpu.VMEM((units, rows, half), BF16),
            pltpu.VMEM((units, rows, block), BF16),
            pltpu.VMEM((CHUNKS, 2, 4, rows, block), BF16),
            pltpu.VMEM((CHUNKS, rows, width), BF16),
            pltpu.VMEM((CHUNKS, rows // 2, width), BF16),
            pltpu.VMEM((CHUNKS, rows // 4, width), BF16),
            pltpu.VMEM((tokens, block), F32),
            pltpu.VMEM((tokens, block), F32),
            pltpu.VMEM((tokens, block), BF16),
            pltpu.VMEM((tokens, tokens), BF16),
            pltpu.VMEM((tokens, 128), F32),
            pltpu.VMEM((prompts // share, share, 128), F32),
            pltpu.VMEM((prompts // share, share, block), F32),
            dma((2 * SLOTS,)), dma((2 * SLOTS,)), dma((2, SLOTS)),
            dma((2,)), dma((4,)), dma((units,)), dma((units,)),
            dma((2 * CHUNKS,)), dma((2 * CHUNKS,)), dma((2 * CHUNKS,)), dma((2 * CHUNKS,)),
            dma((4 * CHUNKS,)), dma((4 * CHUNKS,)),
            dma((3,)), dma((3,)), dma((3,)), dma((3,)),
        ],
        compiler_params=pltpu.CompilerParams(
            collective_id=0, has_side_effects=True, vmem_limit_bytes=VMEM_BYTES
        ),
        name="attribution",
    )(x_clean, x_corr, cotangent, start.reshape(share, 1), partners, w_gate, w_up, w_down)
    return scores, input_grad


def fits(mesh, x_clean, w_gate):
    if mesh.shape["pair"] != 4 or mesh.shape["tensor"] != 4:
        return False
    neurons = w_gate.shape[1] // mesh.shape["tensor"]
    tokens = x_clean.shape[0] // mesh.shape["groups"]
    width = x_clean.shape[1] // mesh.shape["pair"]
    small = tokens <= 512 and width <= 2048 and neurons <= 3584
    return small and neurons % (2 * TILE) == 0 and (neurons // 4) % 128 == 0


def solution(mesh):
    placed = (
        P("groups", "pair"),
        P("groups", "pair"),
        P("groups", "pair"),
        P("pair", "tensor"),
        P("pair", "tensor"),
        P("tensor", "pair"),
        P(("groups", "pair")),
        P(("groups", "pair"), None),
    )

    def run(*args):
        body = fused_body if fits(mesh, args[0], args[3]) else make_body(mesh.shape["pair"])
        return jax.shard_map(
            body,
            mesh=mesh,
            in_specs=placed,
            out_specs=(P(("groups", "pair"), "tensor"), P("groups", "pair")),
            check_vma=False,
        )(*args)

    return run
```

```python
import jax
import jax.numpy as jnp
from jax import lax
from jax.experimental import pallas as pl
from jax.experimental.pallas import tpu as pltpu
from jax.sharding import PartitionSpec as P

SEQ = 16
CHUNKS = 2
STREAMS = 4
VMEM_BYTES = 64 * 2**20 - 2**18


def silu_grad(value):
    sig = jax.nn.sigmoid(value)
    return sig * (1.0 + value * (1.0 - sig))


def make_body(n_pair):
    chips = n_pair // 2
    to_core = [(q, q ^ 1) for q in range(n_pair)]

    def to_chip(shift):
        return [(q, ((q // 2 + shift) % chips) * 2 + q % 2) for q in range(n_pair)]

    def columns(value, at, width):
        return lax.dynamic_slice_in_dim(value, at * width, width, axis=1)

    def body(x_clean, x_corr, cotangent, w_gate, w_up, w_down, start, partners):
        tokens = x_clean.shape[0]
        neurons = w_gate.shape[1]
        half = neurons // 2
        block = half // chips
        index = lax.axis_index("pair")
        core = index % 2
        chip = index // 2
        transposed = (((1,), (1,)), ((), ()))

        def reduce(part):
            arrived = lax.ppermute(columns(part, 1 - core, half), "pair", to_core)
            local = columns(part, core, half).astype(jnp.float32) + arrived.astype(jnp.float32)
            local = local.astype(jnp.bfloat16)
            total = columns(local, chip, block).astype(jnp.float32)
            for shift in range(1, chips):
                piece = columns(local, (chip + shift) % chips, block)
                total = total + lax.ppermute(piece, "pair", to_chip(shift)).astype(jnp.float32)
            return total

        def gather(own):
            rows = own.shape[0]
            mine = jnp.zeros((rows, half), own.dtype)
            mine = lax.dynamic_update_slice_in_dim(mine, own, chip * block, axis=1)
            for shift in range(1, chips):
                piece = lax.ppermute(own, "pair", to_chip(shift))
                source = (chip - shift + chips) % chips
                mine = lax.dynamic_update_slice_in_dim(mine, piece, source * block, axis=1)
            other = lax.ppermute(mine, "pair", to_core)
            first = core == 0
            return jnp.concatenate(
                [jnp.where(first, mine, other), jnp.where(first, other, mine)], axis=1
            )

        def project(left, weight):
            return jnp.dot(left, weight, preferred_element_type=jnp.float32).astype(jnp.bfloat16)

        def project_back(left, weight):
            return lax.dot_general(
                left, weight, transposed, preferred_element_type=jnp.float32
            ).astype(jnp.bfloat16)

        partners_all = lax.all_gather(partners, "pair", axis=0, tiled=True)
        start_all = lax.all_gather(start, "pair", axis=0, tiled=True)

        rows = tokens // CHUNKS
        summed = []
        for k in range(CHUNKS):
            at = slice(k * rows, (k + 1) * rows)
            gate_c = reduce(project(x_clean[at], w_gate))
            up_c = reduce(project(x_clean[at], w_up))
            grad_h = reduce(project_back(cotangent[at], w_down))
            summed.append((gate_c, up_c, grad_h))

        acts, grads, out = [], [], []
        for gate_c, up_c, grad_h in summed:
            silu_c = jax.nn.silu(gate_c)
            acts.append(silu_c * up_c)
            grads.append(grad_h)
            d_gate = gather((grad_h * up_c * silu_grad(gate_c)).astype(jnp.bfloat16))
            d_up = gather((grad_h * silu_c).astype(jnp.bfloat16))
            partial = lax.dot_general(
                d_gate, w_gate, transposed, preferred_element_type=jnp.float32
            )
            partial = partial + lax.dot_general(
                d_up, w_up, transposed, preferred_element_type=jnp.float32
            )
            partial = partial.astype(jnp.bfloat16)
            if out:
                partial, out[-1] = lax.optimization_barrier((partial, out[-1]))
            out.append(lax.psum(partial, "tensor"))
        input_grad = jnp.concatenate(out, axis=0)

        gate_r = reduce(project(x_corr, w_gate))
        up_r = reduce(project(x_corr, w_up))
        act_r = (jax.nn.silu(gate_r) * up_r).astype(jnp.bfloat16)
        act_c = jnp.concatenate(acts, axis=0)
        grad_h = jnp.concatenate(grads, axis=0)

        prompts = tokens // SEQ
        row = jnp.arange(tokens, dtype=jnp.int32)
        used = (partners_all >= 0).astype(jnp.float32)
        mixing = jnp.zeros((tokens, tokens), jnp.float32)
        for slot in range(partners.shape[1]):
            picked = jnp.repeat(partners_all[:, slot], SEQ)
            wanted = jnp.where(picked >= 0, picked * SEQ + row % SEQ, -1)
            mixing = mixing + (wanted[:, None] == row[None, :]).astype(jnp.float32)
        total = jnp.dot(mixing.astype(jnp.bfloat16), act_r, preferred_element_type=jnp.float32)
        count = jnp.repeat(jnp.sum(used, axis=1), SEQ)
        keep = (row % SEQ >= jnp.repeat(start_all, SEQ)).astype(jnp.float32)
        weighted = keep[:, None] * (total - count[:, None] * act_c) * grad_h
        own = jnp.sum(weighted.reshape(prompts, SEQ, block), axis=1) / SEQ
        share = prompts // n_pair
        placed = lax.all_to_all(
            own.reshape(n_pair, share, block), "pair", split_axis=0, concat_axis=0, tiled=True
        )
        placed = placed.reshape(chips, 2, share, block)
        scores = placed.transpose(2, 1, 0, 3).reshape(share, neurons)
        return (scores, input_grad)

    return body


TILE = 256
SLOTS = 2
MESH = pl.DeviceIdType.MESH
F32 = jnp.float32
BF16 = jnp.bfloat16


def fused(
    x_clean, start, partners, x_corr, cotangent, w_gate, w_up, w_down,
    scores, input_grad,
    ring_n, ring_t, ring_b, core_out, core_in, sums, chip_in, grads, part, half_in, quarter_in,
    act_c, grad_h, act_r, mixing, scale, table, own_scores,
    ring_n_sem, ring_t_sem, ring_b_sem, core_out_sem, core_in_sem, chip_out_sem, chip_in_sem,
    dx_out, dx_in, dc_out, dc_in, z_out, z_in, table_out, table_in, score_out, score_in,
    cotangent_in, x_corr_in, late_sem,
):
    tokens, width = x_clean.shape
    rows = tokens // CHUNKS
    neurons = w_gate.shape[1]
    half = neurons // 2
    block = half // 2
    late = {
        2: pltpu.make_async_copy(cotangent, cotangent_in, late_sem.at[0]),
        3 * CHUNKS: pltpu.make_async_copy(x_corr, x_corr_in, late_sem.at[1]),
    }
    share = partners.shape[0]
    prompts = tokens // SEQ
    index = lax.axis_index("pair")
    depth = lax.axis_index("tensor")
    core = lax.rem(index, 2)
    chip = index // 2
    sibling = chip * 2 + (1 - core)
    across = (1 - chip) * 2 + core
    diagonal = (1 - chip) * 2 + (1 - core)
    others = (sibling, across, diagonal)
    odd = lax.rem(depth, 2)
    high = depth // 2
    z_near = high * 2 + (1 - odd)
    z_far = (1 - high) * 2 + odd
    mine = core * 2 + chip
    transposed = (((1,), (1,)), ((), ()))

    def remote(src, dst, send, recv, **where):
        return pltpu.make_async_remote_copy(
            src_ref=src, dst_ref=dst, send_sem=send, recv_sem=recv,
            device_id=where, device_id_type=MESH,
        )

    barrier = pltpu.get_barrier_semaphore()
    for other in others:
        pl.semaphore_signal(barrier, inc=1, device_id={"pair": other}, device_id_type=MESH)
    for other in (z_near, z_far):
        pl.semaphore_signal(barrier, inc=1, device_id={"tensor": other}, device_id_type=MESH)

    units = []
    for k in range(CHUNKS):
        units += [(x_clean, w_gate, False, k), (x_clean, w_up, False, k), (cotangent_in, w_down, True, k)]
    for k in range(CHUNKS):
        units += [(x_corr_in, w_gate, False, k), (x_corr_in, w_up, False, k)]
    tiles = half // TILE

    def tile_copy(u, side, parity, i):
        _, weight, flipped, _ = units[u]
        at = pl.ds(pl.multiple_of(side * half + i * TILE, TILE), TILE)
        slot = parity * SLOTS + lax.rem(i, SLOTS)
        if flipped:
            return pltpu.make_async_copy(weight.at[at, :], ring_t.at[slot], ring_t_sem.at[slot])
        return pltpu.make_async_copy(weight.at[:, at], ring_n.at[slot], ring_n_sem.at[slot])

    stages = [("out", 0)]
    for u in range(len(units)):
        if u + 1 < len(units):
            stages.append(("out", u + 1))
        stages.append(("own", u))
    flow = {"at": 0}

    def side_of(kind):
        return 1 - core if kind == "out" else core

    def prefetch(s):
        if s < len(stages):
            kind, u = stages[s]
            for i in range(SLOTS):
                tile_copy(u, side_of(kind), s % 2, jnp.int32(i)).start()

    def core_copy(u):
        return remote(
            core_out.at[u % 2], core_in.at[u % 4], core_out_sem.at[u % 2], core_in_sem.at[u % 4],
            pair=sibling,
        )

    def chip_copy(u):
        at = pl.ds(pl.multiple_of((1 - chip) * block, 128), block)
        return remote(
            sums.at[u, :, at], chip_in.at[u], chip_out_sem.at[u], chip_in_sem.at[u], pair=across
        )

    def stage():
        s = flow["at"]
        flow["at"] = s + 1
        kind, u = stages[s]
        left, _, flipped, k = units[u]
        prefetch(s + 1)
        if kind == "out" and u >= 2:
            core_copy(u - 2).wait_send()
        if kind == "out" and u in late:
            late[u].wait()
        if kind == "own":
            core_copy(u).wait_recv()

        def step(i, carry):
            tile_copy(u, side_of(kind), s % 2, i).wait()
            slot = (s % 2) * SLOTS + lax.rem(i, SLOTS)
            at = pl.ds(pl.multiple_of(i * TILE, TILE), TILE)
            lhs = left[k * rows:(k + 1) * rows, :]
            if flipped:
                value = lax.dot_general(lhs, ring_t[slot], transposed, preferred_element_type=F32)
            else:
                value = jnp.dot(lhs, ring_n[slot], preferred_element_type=F32)
            if kind == "out":
                core_out[u % 2, :, at] = value.astype(BF16)
            else:
                value = value + core_in[u % 4, :, at].astype(F32)
                sums[u, :, at] = value.astype(BF16)

            @pl.when(i + SLOTS < tiles)
            def _():
                tile_copy(u, side_of(kind), s % 2, i + SLOTS).start()

            return carry

        lax.fori_loop(0, tiles, step, 0)
        if kind == "out":
            core_copy(u).start()

    def run_to(u):
        while ("own", u) not in stages[: flow["at"]]:
            stage()

    own_at = pl.ds(pl.multiple_of(chip * block, 128), block)

    def total(u, at):
        return sums[u, at, own_at].astype(F32) + chip_in[u, at, :].astype(F32)

    def grad_copy(k, a):
        return remote(
            grads.at[k, a, mine], grads.at[k, a, mine], dx_out.at[2 * k + a], dx_in.at[2 * k + a],
            pair=across,
        )

    def grad_share(k, a):
        at = pl.ds(core * 2, 2)
        return remote(
            grads.at[k, a, at], grads.at[k, a, at], dc_out.at[2 * k + a], dc_in.at[2 * k + a],
            pair=sibling,
        )

    def finish_clean(k):
        for u in range(3 * k, 3 * k + 3):
            chip_copy(u).wait_recv()

        def step(i, carry):
            at = pl.ds(pl.multiple_of(i * 16, 16), 16)
            gate, up, grad = (total(3 * k + j, at) for j in range(3))
            sig = jax.nn.sigmoid(gate)
            silu = gate * sig
            grads[k, 0, mine, at, :] = (grad * up * (sig * (1.0 + gate * (1.0 - sig)))).astype(BF16)
            grads[k, 1, mine, at, :] = (grad * silu).astype(BF16)
            place = pl.ds(pl.multiple_of(k * rows + i * 16, 16), 16)
            act_c[place, :] = silu * up
            grad_h[place, :] = grad
            return carry

        lax.fori_loop(0, rows // 16, step, 0)
        for a in range(2):
            grad_copy(k, a).start()

    def finish_corr(k):
        first = 3 * CHUNKS + 2 * k
        for u in (first, first + 1):
            chip_copy(u).wait_recv()

        def step(i, carry):
            at = pl.ds(pl.multiple_of(i * 16, 16), 16)
            gate, up = total(first, at), total(first + 1, at)
            place = pl.ds(pl.multiple_of(k * rows + i * 16, 16), 16)
            act_r[place, :] = (gate * jax.nn.sigmoid(gate) * up).astype(BF16)
            return carry

        lax.fori_loop(0, rows // 16, step, 0)

    def back_copy(a, i):
        slot = lax.rem(i, SLOTS)
        at = pl.ds(pl.multiple_of(i * TILE, TILE), TILE)
        weight = (w_gate, w_up)[a]
        return pltpu.make_async_copy(
            weight.at[at, :], ring_b.at[a, slot], ring_b_sem.at[a, slot]
        )

    def back(k):
        steps = width // TILE
        for i in range(SLOTS):
            for a in range(2):
                back_copy(a, jnp.int32(i)).start()
        for a in range(2):
            grad_copy(k, a).wait_recv()
            grad_share(k, a).start()
        for a in range(2):
            grad_share(k, a).wait_recv()

        def step(i, carry):
            slot = lax.rem(i, SLOTS)
            value = jnp.zeros((rows, TILE), F32)
            for a in range(2):
                back_copy(a, i).wait()
                for b in range(4):
                    value = value + lax.dot_general(
                        grads[k, a, b], ring_b[a, slot, :, b * block:(b + 1) * block],
                        transposed, preferred_element_type=F32,
                    )
            part[k, :, pl.ds(pl.multiple_of(i * TILE, TILE), TILE)] = value.astype(BF16)

            @pl.when(i + SLOTS < steps)
            def _():
                for a in range(2):
                    back_copy(a, i + SLOTS).start()

            return carry

        for h in range(STREAMS):
            lax.fori_loop(h * steps // STREAMS, (h + 1) * steps // STREAMS, step, 0)
            z_copy(k, 0, h).start()

    half_rows = rows // 2
    quarter_rows = rows // 4

    stream = width // STREAMS

    def z_copy(k, n, h):
        which = (k * STREAMS + h) * 4 + n
        sems = z_out.at[which], z_in.at[which]
        cols = pl.ds(h * stream, stream)
        if n == 0:
            at = pl.ds(pl.multiple_of((1 - odd) * half_rows, 16), half_rows)
            return remote(part.at[k, at, cols], half_in.at[k, :, cols], *sems, tensor=z_near)
        if n == 1:
            at = pl.ds(
                pl.multiple_of(odd * half_rows + (1 - high) * quarter_rows, 16), quarter_rows
            )
            return remote(part.at[k, at, cols], quarter_in.at[k, :, cols], *sems, tensor=z_far)
        if n == 2:
            at = pl.ds(
                pl.multiple_of(k * rows + odd * half_rows + high * quarter_rows, 16), quarter_rows
            )
            return remote(input_grad.at[at, cols], input_grad.at[at, cols], *sems, tensor=z_far)
        at = pl.ds(pl.multiple_of(k * rows + odd * half_rows, 16), half_rows)
        return remote(input_grad.at[at, cols], input_grad.at[at, cols], *sems, tensor=z_near)

    def z_step(k, n, h):
        z_copy(k, n, h).wait_recv()
        cols = pl.ds(h * stream, stream)
        if n == 0:

            def step(i, carry):
                at = pl.ds(pl.multiple_of(odd * half_rows + i * 16, 16), 16)
                here = pl.ds(pl.multiple_of(i * 16, 16), 16)
                part[k, at, cols] = (
                    part[k, at, cols].astype(F32) + half_in[k, here, cols].astype(F32)
                ).astype(BF16)
                return carry

            lax.fori_loop(0, half_rows // 16, step, 0)
        if n == 1:

            def step(i, carry):
                local = odd * half_rows + high * quarter_rows + i * 16
                at = pl.ds(pl.multiple_of(local, 16), 16)
                place = pl.ds(pl.multiple_of(k * rows + local, 16), 16)
                here = pl.ds(pl.multiple_of(i * 16, 16), 16)
                input_grad[place, cols] = (
                    part[k, at, cols].astype(F32) + quarter_in[k, here, cols].astype(F32)
                ).astype(BF16)
                return carry

            lax.fori_loop(0, quarter_rows // 16, step, 0)
        if n < 3:
            z_copy(k, n + 1, h).start()

    def table_copy(n):
        return remote(
            table.at[index], table.at[index], table_out.at[n], table_in.at[n], pair=others[n]
        )

    def score_copy(n):
        at = pl.ds(pl.multiple_of(mine * block, 128), block)
        return remote(
            own_scores.at[others[n]], scores.at[:, at], score_out.at[n], score_in.at[n],
            pair=others[n],
        )

    prefetch(0)
    for copy in late.values():
        copy.start()
    lane = lax.broadcasted_iota(jnp.int32, (share, 128), 1)
    counts = jnp.zeros((share, 128), F32)
    used = jnp.zeros((share, 1), F32)
    for slot in range(partners.shape[1]):
        picked = partners[:, slot:slot + 1]
        counts = counts + (lane == picked).astype(F32)
        used = used + (picked >= 0).astype(F32)
    counts = jnp.where(lane == 126, start[...].astype(F32), counts)
    table[index] = jnp.where(lane == 127, used, counts)
    pl.semaphore_wait(barrier, 5)
    for n in range(3):
        table_copy(n).start()

    def send(*which):
        for u in which:
            run_to(u)
            chip_copy(u).start()

    def z_all(k, n):
        for h in range(STREAMS):
            z_step(k, n, h)

    first_corr = 3 * CHUNKS
    send(0, 1, 2, 3)
    finish_clean(0)
    send(4, 5)

    for n in range(3):
        table_copy(n).wait_recv()
    spread = (
        lax.broadcasted_iota(jnp.int32, (tokens, prompts), 0) // SEQ
        == lax.broadcasted_iota(jnp.int32, (tokens, prompts), 1)
    ).astype(BF16)
    by_row = jnp.dot(
        spread, table[...].reshape(prompts, 128).astype(BF16), preferred_element_type=F32
    )
    position = lax.rem(lax.broadcasted_iota(jnp.int32, (tokens, 1), 0), SEQ)
    keep = (position.astype(F32) >= by_row[:, 126:127]).astype(F32)
    scale[...] = jnp.broadcast_to(keep * by_row[:, 127:128], (tokens, 128))
    widen = (
        lax.broadcasted_iota(jnp.int32, (128, tokens), 1) // SEQ
        == lax.broadcasted_iota(jnp.int32, (128, tokens), 0)
    ).astype(BF16)
    wide = jnp.dot((keep * by_row).astype(BF16), widen, preferred_element_type=F32)
    same = position == lax.rem(lax.broadcasted_iota(jnp.int32, (tokens, tokens), 1), SEQ)
    mixing[...] = jnp.where(same, wide, 0.0).astype(BF16)

    back(0)
    run_to(first_corr)
    z_all(0, 0)
    run_to(first_corr + 1)
    z_all(0, 1)
    finish_clean(1)
    send(first_corr, first_corr + 1, first_corr + 2)
    z_all(0, 2)
    send(first_corr + 3)
    back(1)
    z_all(1, 0)
    finish_corr(0)
    z_all(1, 1)
    z_all(1, 2)
    finish_corr(1)

    span = share * SEQ

    def score_step(i, carry):
        at = pl.ds(pl.multiple_of(i * span, span), span)
        mixed = jnp.dot(mixing[at, :], act_r[...], preferred_element_type=F32)
        value = (mixed - scale[at, 0:1] * act_c[at, :]) * grad_h[at, :]
        own_scores[i] = jnp.sum(value.reshape(share, SEQ, block), axis=1) * (1.0 / SEQ)
        return carry

    lax.fori_loop(0, prompts // share, score_step, 0)
    for n in range(3):
        score_copy(n).start()
    scores[:, pl.ds(pl.multiple_of(mine * block, 128), block)] = own_scores[index]

    for k in range(CHUNKS):
        for h in range(STREAMS):
            z_copy(k, 3, h).wait_recv()
    for n in range(3):
        score_copy(n).wait()
        table_copy(n).wait_send()
    for u in (len(units) - 2, len(units) - 1):
        core_copy(u).wait_send()
    for u in range(len(units)):
        chip_copy(u).wait_send()
    for k in range(CHUNKS):
        for a in range(2):
            grad_copy(k, a).wait_send()
            grad_share(k, a).wait_send()
        for n in range(4):
            for h in range(STREAMS):
                z_copy(k, n, h).wait_send()


def fused_body(x_clean, x_corr, cotangent, w_gate, w_up, w_down, start, partners):
    tokens, width = x_clean.shape
    neurons = w_gate.shape[1]
    rows, half = tokens // CHUNKS, neurons // 2
    block = half // 2
    share = start.shape[0]
    prompts = tokens // SEQ
    units = 5 * CHUNKS
    vmem = pl.BlockSpec(memory_space=pltpu.VMEM)
    anywhere = pl.BlockSpec(memory_space=pl.ANY)
    dma = pltpu.SemaphoreType.DMA
    scores, input_grad = pl.pallas_call(
        fused,
        out_shape=(
            jax.ShapeDtypeStruct((share, neurons), F32),
            jax.ShapeDtypeStruct((tokens, width), BF16),
        ),
        in_specs=[vmem] * 3 + [anywhere] * 5,
        out_specs=(vmem, vmem),
        scratch_shapes=[
            pltpu.VMEM((2 * SLOTS, width, TILE), BF16),
            pltpu.VMEM((2 * SLOTS, TILE, width), BF16),
            pltpu.VMEM((2, SLOTS, TILE, neurons), BF16),
            pltpu.VMEM((2, rows, half), BF16),
            pltpu.VMEM((4, rows, half), BF16),
            pltpu.VMEM((units, rows, half), BF16),
            pltpu.VMEM((units, rows, block), BF16),
            pltpu.VMEM((CHUNKS, 2, 4, rows, block), BF16),
            pltpu.VMEM((CHUNKS, rows, width), BF16),
            pltpu.VMEM((CHUNKS, rows // 2, width), BF16),
            pltpu.VMEM((CHUNKS, rows // 4, width), BF16),
            pltpu.VMEM((tokens, block), F32),
            pltpu.VMEM((tokens, block), F32),
            pltpu.VMEM((tokens, block), BF16),
            pltpu.VMEM((tokens, tokens), BF16),
            pltpu.VMEM((tokens, 128), F32),
            pltpu.VMEM((prompts // share, share, 128), F32),
            pltpu.VMEM((prompts // share, share, block), F32),
            dma((2 * SLOTS,)), dma((2 * SLOTS,)), dma((2, SLOTS)),
            dma((2,)), dma((4,)), dma((units,)), dma((units,)),
            dma((2 * CHUNKS,)), dma((2 * CHUNKS,)), dma((2 * CHUNKS,)), dma((2 * CHUNKS,)),
            dma((4 * CHUNKS * STREAMS,)), dma((4 * CHUNKS * STREAMS,)),
            dma((3,)), dma((3,)), dma((3,)), dma((3,)),
            pltpu.VMEM((tokens, width), BF16), pltpu.VMEM((tokens, width), BF16), dma((2,)),
        ],
        compiler_params=pltpu.CompilerParams(
            collective_id=0, has_side_effects=True, vmem_limit_bytes=VMEM_BYTES
        ),
        name="attribution",
    )(x_clean, start.reshape(share, 1), partners, x_corr, cotangent, w_gate, w_up, w_down)
    return scores, input_grad


def fits(mesh, x_clean, w_gate):
    if mesh.shape["pair"] != 4 or mesh.shape["tensor"] != 4:
        return False
    neurons = w_gate.shape[1] // mesh.shape["tensor"]
    tokens = x_clean.shape[0] // mesh.shape["groups"]
    width = x_clean.shape[1] // mesh.shape["pair"]
    small = tokens <= 512 and width <= 2048 and neurons <= 3584
    return small and neurons % (2 * TILE) == 0 and (neurons // 4) % 128 == 0


def solution(mesh):
    placed = (
        P("groups", "pair"),
        P("groups", "pair"),
        P("groups", "pair"),
        P("pair", "tensor"),
        P("pair", "tensor"),
        P("tensor", "pair"),
        P(("groups", "pair")),
        P(("groups", "pair"), None),
    )

    def run(*args):
        body = fused_body if fits(mesh, args[0], args[3]) else make_body(mesh.shape["pair"])
        return jax.shard_map(
            body,
            mesh=mesh,
            in_specs=placed,
            out_specs=(P(("groups", "pair"), "tensor"), P("groups", "pair")),
            check_vma=False,
        )(*args)

    return run
```
